32 devices in a mesh: expert: 8 (over z, y), tensor: 4 (over x, core).
Axes of the slice: x: 2, y: 2, z: 4, core: 2. Of those that a mesh axis runs over, the one named last changes fastest.
Arguments:
- tokens: bfloat16 [32768, 1024], P(('expert', 'tensor')), may hold values from -6 to 6
- routes: int32 [32768, 1], P(('expert', 'tensor')), may hold values from 0 to 15; in each aligned block of 1024 rows (0 to 1023, 1024 to 2047, ...) at most 128 rows name the same one
- cotangent: bfloat16 [32768, 1024], P(('expert', 'tensor')), may hold values from -6 to 6
- ln_gain: bfloat16 [16, 1024], P('expert'), may hold values from 0.099609375 to 1.8984375
- layer_norm_bias: bfloat16 [16, 1024], P('expert'), may hold values from -1.796875 to 1.796875
- centroid: bfloat16 [16, 1024], P('expert'), may hold values from -0.119628906 to 0.119628906
- w_in: bfloat16 [16, 1024, 4096], P('expert', None, 'tensor'), may hold values from -0.1875 to 0.1875
- w_out: bfloat16 [16, 4096, 1024], P('expert', 'tensor'), may hold values from -0.1875 to 0.1875
Outputs:
- layer_out: bfloat16 [32768, 1024], P(('expert', 'tensor'))
- tokens_grad: float32 [32768, 1024], P(('expert', 'tensor'))
- gain_grad: float32 [16, 1024], P('expert')
- bias_grad: float32 [16, 1024], P('expert')
- centroid_grad: float32 [16, 1024], P('expert')
- w_in_grad: float32 [16, 1024, 4096], P('expert', None, 'tensor')
- w_out_grad: float32 [16, 4096, 1024], P('expert', 'tensor')
The draws below stay inside these ranges and needn't reach their ends.
Inputs may be any that keep to these rules, and one draw needn't show every extreme that they name: `routes`: of the tokens of one device (aligned blocks of 1024 rows) at most 128 name one expert; some expert receives exactly 128 from some device in every draw.
All inputs are finite; a program needn't handle non-finite values.
Results may differ from the reference program's by a relative error of at most 0.0063.
Values may be sent and summed in bfloat16 or wider, within the bound.
No kernel may reach another device: no remote copies, remote signals or barrier semaphores. Data moves between devices by JAX's collectives and lax.ppermute only.
A program may use at most 256 MiB of HBM per device.

```python
import math
import jax
import jax.numpy as jnp
import numpy as np
from jax import lax

D = 1024
FF = 4096
TOK_DEV = 1024
EXPERTS = 16
TOKENS = 32768
CAP = 128


def block_levels(rng, shape, shards, smallest, high):
    loudness, own = 1.0, jax.random.fold_in(rng, 6)
    for dim, blocks in shards:
        steps = jnp.exp(jax.random.uniform(jax.random.fold_in(own, dim), (blocks,), jnp.float32, smallest / len(shards), high / len(shards)))
        loudness = loudness * jnp.repeat(steps, shape[dim] // blocks).reshape([-1 if axis == dim else 1 for axis in range(len(shape))])
    return loudness


def shared_out(stream_key, own, number, rows, amount, top, limit, slope):
    sequence = jax.random.permutation(stream_key, amount)
    heavy_load, usual = load_shares(amount, rows * top, limit, slope, True), load_shares(amount, rows * top, limit, slope, False)
    places = jnp.arange(amount)

    def named(lengths, rotation):
        used = int((lengths > 0).sum())
        fixed = max(1, used // 4)
        passed = fixed + (places - fixed + rotation * (used - fixed)) % max(1, amount - fixed)
        return jnp.zeros((amount,), jnp.int32).at[sequence[jnp.where(places < fixed, places, passed)]].set(jnp.asarray(lengths, jnp.int32))

    lengths = jnp.where(number % 4 == 0, named(heavy_load, number // 4), named(usual, number - number // 4 - 1))
    mixed = jax.random.permutation(jax.random.fold_in(own, 3), amount)
    giver, taker = mixed[0:amount // 2 * 2:2], mixed[1:amount // 2 * 2:2]
    slack = jnp.minimum(lengths[giver] - 1, limit - lengths[taker]) // 2
    slack = jnp.where((giver == sequence[0]) | (taker == sequence[0]) | (lengths[taker] == 0), 0, jnp.maximum(slack, 0))
    passed = jax.random.randint(jax.random.fold_in(own, 4), (amount // 2,), 0, 1 << 20) % (slack + 1)
    lengths = lengths.at[giver].add(-passed).at[taker].add(passed)
    labels = jnp.searchsorted(jnp.cumsum(lengths), jnp.arange(rows * top), side="right").astype(jnp.int32)
    table = labels.reshape(top, rows).T
    table = table[jax.random.permutation(jax.random.fold_in(own, 1), rows)]
    rotation = jax.random.randint(jax.random.fold_in(own, 2), (rows, 1), 0, top)
    return jnp.take_along_axis(table, (jnp.arange(top)[None, :] + rotation) % top, axis=1)


def load_shares(amount, total, bound, slope, full):
    loads = [(1 << 20) // math.isqrt(grade ** slope) + 1 for grade in range(1, amount + 1)]
    largest = bound if full else min(bound, max(-(-total // amount), total * loads[0] // sum(loads)))
    least = 1 if total - largest >= amount - 1 else 0
    holding, rest = [largest] + [least] * (amount - 1), total - largest - least * (amount - 1)
    while rest > 0:
        movable = [i for i in range(1, amount) if holding[i] < largest] or [i for i in range(1, amount) if holding[i] < bound]
        whole, left = sum([loads[i] for i in movable]), rest
        for i in movable:
            more = min(bound - holding[i], max(1, left * loads[i] // whole), rest)
            holding[i] = holding[i] + more
            rest = rest - more
    return np.array(holding)


def normal_values(key, extent, spread, limit, split=(), kind=jnp.bfloat16):
    level = block_levels(key, extent, split, -0.22, 0.18) if split else 1.0
    drawn = jax.random.normal(key, extent, jnp.float32) * spread * level
    return jnp.minimum(jnp.maximum(drawn, -limit), limit).astype(kind)


def setup_inputs(seed: int = 0) -> dict:
    streams_of = jax.random.split(jax.random.key(seed), 9)
    tokens = normal_values(streams_of[0], (TOKENS, D), 1.0, 6.0, ((0, 32),))
    routes_keys = jax.random.split(jax.random.fold_in(streams_of[1], 1), TOKENS // TOK_DEV)
    routes_turns = jax.random.permutation(jax.random.fold_in(streams_of[1], 3), TOKENS // TOK_DEV)
    routes = jax.vmap(lambda own, number: shared_out(jax.random.fold_in(streams_of[1], 2), own, number, TOK_DEV, EXPERTS, 1, CAP, 1))(routes_keys, routes_turns).reshape((TOKENS, 1))
    cotangent = normal_values(streams_of[2], (TOKENS, D), 1.0, 6.0, ((0, 32),))
    ln_gain = jnp.clip(1.0 + 0.18 * jax.random.normal(streams_of[3], (EXPERTS, D), jnp.float32), 0.099609375, 1.8984375).astype(jnp.bfloat16)
    layer_norm_bias = normal_values(streams_of[4], (EXPERTS, D), 0.3, 1.796875, ((0, 8),))
    centroid = normal_values(streams_of[5], (EXPERTS, D), 0.02, 0.119628906, ((0, 8),))
    w_in = normal_values(streams_of[6], (EXPERTS, D, FF), D ** -0.5, 0.1875, ((0, 8), (2, 4)))
    w_out = normal_values(streams_of[7], (EXPERTS, FF, D), (FF // 4) ** -0.5, 0.1875, ((0, 8), (1, 4)))
    return {"tokens": tokens, "routes": routes, "cotangent": cotangent, "ln_gain": ln_gain, "layer_norm_bias": layer_norm_bias, "centroid": centroid, "w_in": w_in, "w_out": w_out}


@jax.custom_vjp
def low(v):
    return lax.optimization_barrier(v.astype(jnp.bfloat16)).astype(jnp.float32)

@jax.custom_vjp
def low_back(v):
    return v

def low_keep(v):
    return (low(v), None)

def low_pass(kept, grad):
    return (grad,)

def back_keep(v):
    return (v, None)

def back_low(kept, grad):
    return (low(grad),)
low.defvjp(low_keep, low_pass)
low_back.defvjp(back_keep, back_low)
epsilon = 1e-05

def expert_block(pieces):
    batch, gain, bias, center, first, second = pieces
    row_mean = lax.optimization_barrier(jnp.mean(batch, axis=-1, keepdims=True))
    centered_rows = batch - row_mean
    variance = lax.optimization_barrier(jnp.mean(centered_rows * centered_rows, axis=-1, keepdims=True))
    normed_rows = low(centered_rows * lax.rsqrt(variance + epsilon) * gain[None, :] + bias[None, :])
    preact = low_back(jnp.dot(normed_rows, first, precision=lax.Precision.HIGHEST))
    hidden = low(jax.nn.gelu(preact, approximate=False))
    mixed = low_back(jnp.dot(hidden, second, precision=lax.Precision.HIGHEST))
    gate_val = jax.nn.sigmoid(jnp.dot(batch, center, precision=lax.Precision.HIGHEST))
    return low(gate_val[:, None] * mixed)

def reference(tokens, routes, cotangent, ln_gain, layer_norm_bias, centroid, w_in, w_out):
    targets = routes[:, 0].astype(jnp.int32)
    onehot = (targets[:, None] == jnp.arange(EXPERTS, dtype=jnp.int32)[None, :]).astype(jnp.int32)
    blocked = onehot.reshape(TOKENS // TOK_DEV, TOK_DEV, EXPERTS)
    ranks = lax.optimization_barrier(jnp.sum(jnp.cumsum(blocked, axis=1) * blocked, axis=2)).reshape(TOKENS) - 1
    source = jnp.arange(TOKENS, dtype=jnp.int32) // TOK_DEV
    position = (source * CAP + ranks).astype(jnp.int32)
    slots = TOKENS // TOK_DEV * CAP

    def forward(inputs, gain, bias, center, first, second):
        buffer = jnp.zeros((EXPERTS, slots, D), inputs.dtype).at[targets, position].set(inputs)
        buffer = low_back(buffer)
        results = lax.map(jax.checkpoint(expert_block), (buffer, gain, bias, center, first, second))
        return inputs + results[targets, position]
    floats = (tokens.astype(jnp.float32), ln_gain.astype(jnp.float32), layer_norm_bias.astype(jnp.float32), centroid.astype(jnp.float32), w_in.astype(jnp.float32), w_out.astype(jnp.float32))
    value, pullback = jax.vjp(forward, *floats)
    grads = pullback(cotangent.astype(jnp.float32))
    return (value.astype(jnp.bfloat16), grads[0], grads[1], grads[2], grads[3], grads[4], grads[5])
```

```python
import jax
import jax.numpy as jnp
from jax import lax
from jax.sharding import Mesh
from jax.sharding import PartitionSpec as P

epsilon = 1e-05
F32 = jnp.float32
BF16 = jnp.bfloat16


def per_device(tokens, routes, cotangent, ln_gain, layer_norm_bias, centroid, w_in, w_out):
    groups, halves, subs = (lax.axis_size(a) for a in ("expert", "half", "sub"))
    half = lax.axis_index("half")
    experts = groups * halves
    count, width = tokens.shape
    capacity = 2 * count // experts
    targets = routes[:, 0]

    onehot = targets[:, None] == jnp.arange(experts, dtype=jnp.int32)[None, :]
    order = jnp.arange(count, dtype=jnp.int32)
    earlier = (order[:, None] >= order[None, :]).astype(BF16)
    ranks = jnp.dot(earlier, onehot.astype(BF16), preferred_element_type=F32)
    ranks = jnp.sum(jnp.where(onehot, ranks, 0.0), axis=1).astype(jnp.int32) - 1
    slot = targets * capacity + ranks
    slots = jnp.arange(experts * capacity, dtype=jnp.int32)

    def place(values):
        chosen = (slots[:, None] == slot[None, :]).astype(BF16)
        return jnp.dot(chosen, values, preferred_element_type=F32).astype(BF16)

    def unplace(arrived):
        chosen = (slot[:, None] == slots[None, :]).astype(BF16)
        return jnp.dot(chosen, arrived, preferred_element_type=F32)

    def exchange(rows):
        rows = rows.reshape(experts, capacity, width)
        return lax.all_to_all(
            rows, ("expert", "half"), split_axis=0, concat_axis=0, tiled=True
        ).reshape(experts * capacity, width)

    def over(axis, value):
        size = lax.axis_size(axis)
        return lax.ppermute(value, axis, [(i, size - 1 - i) for i in range(size)])

    def pick(stacked, index):
        return lax.dynamic_index_in_dim(stacked, index, 0, keepdims=False)

    def blocks_of(weight):
        own, send = pick(weight, half), pick(weight, 1 - half)
        beside = over("half", send)
        return [own, over("sub", own), beside, over("sub", beside)]

    x = exchange(place(tokens)).astype(F32)
    ins, outs = blocks_of(w_in), blocks_of(w_out)
    dy = exchange(place(cotangent)).astype(F32)

    gain = pick(ln_gain, half).astype(F32)[None, :]
    bias = pick(layer_norm_bias, half).astype(F32)[None, :]
    center = pick(centroid, half).astype(F32)[None, :]
    centered = x - jnp.mean(x, axis=-1, keepdims=True)
    inverse = lax.rsqrt(jnp.mean(centered * centered, axis=-1, keepdims=True) + epsilon)
    xhat = centered * inverse
    normed = (xhat * gain + bias).astype(BF16)
    gate = jax.nn.sigmoid(jnp.sum(x * center, axis=-1, keepdims=True))

    hiddens, slopes = [], []
    mixed = 0.0
    for first, second in zip(ins, outs):
        z = jnp.dot(normed, first, preferred_element_type=F32)
        cumul = 0.5 * (1.0 + lax.erf(z * 0.7071067811865476))
        density = jnp.exp(-0.5 * z * z) * 0.3989422804014327
        hidden = (z * cumul).astype(BF16)
        hiddens.append(hidden)
        slopes.append((cumul + z * density).astype(BF16))
        mixed = mixed + jnp.dot(hidden, second, preferred_element_type=F32)
    returned = exchange((gate * mixed).astype(BF16))

    logit_grad = jnp.sum(dy * mixed, axis=-1, keepdims=True) * gate * (1.0 - gate)
    mixed_grad = (gate * dy).astype(BF16)
    rows_in = (((0,), (0,)), ((), ()))
    last = (((1,), (1,)), ((), ()))
    pre_grads = []
    normed_grad = 0.0
    for first, second, slope in zip(ins, outs, slopes):
        hidden_grad = lax.dot_general(mixed_grad, second, last, preferred_element_type=F32)
        pre_grad = (hidden_grad * slope.astype(F32)).astype(BF16)
        pre_grads.append(pre_grad)
        normed_grad = normed_grad + lax.dot_general(
            pre_grad, first, last, preferred_element_type=F32
        )
    u = normed_grad * gain
    expert_grad = (
        inverse
        * (u - jnp.mean(u, axis=-1, keepdims=True) - xhat * jnp.mean(u * xhat, axis=-1, keepdims=True))
        + logit_grad * center
    )
    back = exchange(expert_grad.astype(BF16))

    def shared(parts):
        kept = parts[0] + over("sub", parts[1].astype(BF16)).astype(F32)
        sent = parts[2] + over("sub", parts[3].astype(BF16)).astype(F32)
        got = over("half", sent.astype(BF16)).astype(F32)
        return jnp.stack([jnp.where(half == i, kept, got) for i in range(2)])

    out_wgrad = shared(
        [lax.dot_general(h, mixed_grad, rows_in, preferred_element_type=F32) for h in hiddens]
    )
    in_wgrad = shared(
        [lax.dot_general(normed, p, rows_in, preferred_element_type=F32) for p in pre_grads]
    )
    small = jnp.stack(
        [
            jnp.sum(normed_grad * xhat, axis=0),
            jnp.sum(normed_grad, axis=0),
            jnp.sum(logit_grad * x, axis=0),
        ]
    )
    small = jnp.where((jnp.arange(halves) == half)[:, None, None], small[None], 0.0)
    small = lax.psum(small, ("half", "sub"))
    layer_out = (tokens.astype(F32) + unplace(returned)).astype(BF16)
    tokens_grad = cotangent.astype(F32) + unplace(back)
    return (layer_out, tokens_grad, small[:, 0], small[:, 1], small[:, 2], in_wgrad, out_wgrad)


def solution(mesh):
    groups, tensor = mesh.shape["expert"], mesh.shape["tensor"]
    halves = 2
    split = Mesh(
        mesh.devices.reshape(groups, halves, tensor // halves), ("expert", "half", "sub")
    )
    rows, within = P(("expert", "half", "sub"), None), P("expert", None)
    columns = P("expert", None, ("half", "sub"))
    depth = P("expert", ("half", "sub"), None)
    return jax.shard_map(
        per_device,
        mesh=split,
        in_specs=(rows, rows, rows, within, within, within, columns, depth),
        out_specs=(rows, rows, within, within, within, columns, depth),
        check_vma=False,
    )
```

```python
import functools

import jax
import jax.numpy as jnp
from jax import lax
from jax.experimental import pallas as pl
from jax.experimental.pallas import tpu as pltpu
from jax.sharding import Mesh
from jax.sharding import PartitionSpec as P

epsilon = 1e-05
F32 = jnp.float32
BF16 = jnp.bfloat16
LAST = (((1,), (1,)), ((), ()))
ROWS = (((0,), (0,)), ((), ()))
VMEM_LIMIT = 58 * 2**20
TILE = 512


def product(a, b, dims=(((1,), (0,)), ((), ()))):
    return lax.dot_general(a, b, dims, preferred_element_type=F32)


def standardize(x):
    centered = x - jnp.mean(x, axis=-1, keepdims=True)
    inverse = lax.rsqrt(jnp.mean(centered * centered, axis=-1, keepdims=True) + epsilon)
    return centered * inverse, inverse


def steps_of(weights):
    for first, second in weights:
        step = min(TILE, first.shape[1]) if first.shape[1] % TILE == 0 else first.shape[1]
        for start in range(0, first.shape[1], step):
            yield first[:, start : start + step], second[start : start + step, :]


def through(normed, weights, hidden_ref, slope_ref):
    total, at = None, 0
    for first, second in steps_of(weights):
        z = product(normed, first)
        cumul = 0.5 * (1.0 + lax.erf(z * 0.7071067811865476))
        density = jnp.exp(-0.5 * z * z) * 0.3989422804014327
        hidden = (z * cumul).astype(BF16)
        hidden_ref[:, at : at + z.shape[1]] = hidden
        slope_ref[:, at : at + z.shape[1]] = (cumul + z * density).astype(BF16)
        part = product(hidden, second)
        total = part if total is None else total + part
        at += z.shape[1]
    return total


def paired(refs):
    return list(zip(refs[::2], refs[1::2]))


def forward_near(x, gain, bias, center, *rest):
    weights, (normed, hidden, slope, mixed, gates) = paired(rest[:-6]), rest[-5:]
    values = x[...].astype(F32)
    rows = (standardize(values)[0] * gain[...] + bias[...]).astype(BF16)
    normed[...] = rows
    mixed[...] = through(rows, weights, hidden, slope)
    gate = jax.nn.sigmoid(jnp.sum(values * center[...], axis=-1, keepdims=True))
    gates[...] = jnp.broadcast_to(gate, gates.shape)


def forward_more(rows, near, *rest):
    weights, (hidden, slope, mixed) = paired(rest[:-3]), rest[-3:]
    mixed[...] = near[...] + through(rows[...], weights, hidden, slope)


def forward_last(rows, near, gates, first, second, kept_hidden, kept_slope, hidden, slope, gated):
    del kept_hidden, kept_slope
    whole = near[...] + through(rows[...], [(first, second)], hidden, slope)
    gated[...] = (gates[:, :1] * whole).astype(BF16)


def backward(x, dy, gated, s1, s2, gates, gain, center, *rest):
    weights, (g1, g2, expert_grad, sums) = paired(rest[:-4]), rest[-4:]
    rows = x[...].astype(F32)
    gate = gates[:, :1]
    upper = dy[...].astype(F32)
    mixed_grad = (gate * upper).astype(BF16)
    total, at = None, 0
    for first, second in steps_of(weights):
        slope, grad, start = (s1, g1, at) if at < s1.shape[1] else (s2, g2, at - s1.shape[1])
        hidden_grad = product(mixed_grad, second, LAST)
        columns = pl.ds(start, second.shape[0])
        pre_grad = (hidden_grad * slope[:, columns].astype(F32)).astype(BF16)
        grad[:, columns] = pre_grad
        added = product(pre_grad, first, LAST)
        total = added if total is None else total + added
        at += second.shape[0]
    xhat, inverse = standardize(rows)
    logit_grad = jnp.sum(upper * gated[...].astype(F32), axis=-1, keepdims=True) * (1.0 - gate)
    u = total * gain[...]
    expert_grad[...] = (
        inverse
        * (u - jnp.mean(u, axis=-1, keepdims=True) - xhat * jnp.mean(u * xhat, axis=-1, keepdims=True))
        + logit_grad * center[...]
    ).astype(BF16)

    @pl.when(pl.program_id(0) == 0)
    def _():
        sums[...] = jnp.zeros_like(sums)

    sums[0:1, :] += jnp.sum(total * xhat, axis=0, keepdims=True)
    sums[1:2, :] += jnp.sum(total, axis=0, keepdims=True)
    sums[2:3, :] += jnp.sum(logit_grad * rows, axis=0, keepdims=True)


def call(kernel, name, steps, ins, outs, **more):
    def spec(shape, block, index):
        if block == "out":
            return pl.BlockSpec(memory_space=pl.ANY)
        if block is None:
            return pl.BlockSpec(shape, lambda *_: (0,) * len(shape), pipeline_mode=pl.Buffered(1))
        return pl.BlockSpec(block, index)

    return pl.pallas_call(
        kernel,
        grid=(steps,),
        in_specs=[spec(a.shape, block, index) for a, block, index in ins],
        out_specs=[pl.BlockSpec(block, index) for _, _, block, index in outs],
        out_shape=[jax.ShapeDtypeStruct(shape, dtype) for shape, dtype, _, _ in outs],
        compiler_params=pltpu.CompilerParams(vmem_limit_bytes=VMEM_LIMIT),
        cost_estimate=pl.CostEstimate(flops=1000, transcendentals=0, bytes_accessed=1000),
        name=name,
        **more,
    )(*[a for a, _, _ in ins])


def tiles(array, tile):
    return array, (tile, array.shape[1]), lambda i: (i, 0)


def rows_out(shape, dtype, tile):
    return shape, dtype, (tile, shape[1]), lambda i: (i, 0)


def whole(array):
    return array, None, None


def weight_grad(left, right, units, width, dtype, name, beside=None, apart=False):
    (a, i), (b, j) = left, right
    tile = min(TILE, units)
    steps = units // tile

    def kernel(a, b, *rest):
        total = product(a[...], b[...], ROWS).astype(dtype)
        if not apart and beside is None:
            rest[0][...] = total
        for n in range(steps if apart or beside is not None else 0):

            @pl.when(pl.program_id(0) == n)
            def _():
                if apart:
                    rest[n][...] = total
                else:
                    rest[-1][0] = total
                    rest[-1][1] = rest[n][...]

    ins = [
        (a, (a.shape[0], tile), lambda n: (0, i * steps + n)),
        (b, (b.shape[0], width), lambda n: (0, j)),
    ]
    if apart:
        return call(kernel, name, steps, ins, [((tile, width), dtype, (tile, width), lambda n: (0, 0))] * steps)
    if beside is None:
        return call(kernel, name, steps, ins, [rows_out((units, width), dtype, tile)])[0]
    out = (2, units, width), dtype, (2, tile, width), lambda n: (0, n, 0)
    return call(kernel, name, steps, ins + [whole(p) for p in beside], [out])[0]


def first_weight_grad(hidden, dy, gates, units, name):
    count, width = dy.shape
    tile = min(TILE, units)

    def kernel(a, dy, gates, out, mixed_grad):
        @pl.when(pl.program_id(0) == 0)
        def _():
            mixed_grad[...] = (gates[:, :1] * dy[...].astype(F32)).astype(BF16)

        out[...] = product(a[...], mixed_grad[...], ROWS).astype(BF16)

    return call(
        kernel,
        name,
        units // tile,
        [(hidden, (count, tile), lambda n: (0, n)), whole(dy), whole(gates)],
        [rows_out((units, width), BF16, tile), ((count, width), BF16, (count, width), lambda n: (0, 0))],
    )


def joined(half, own, beside, across, name):
    count, width = own.shape
    tile = min(256, count)

    def kernel(half, own, beside, *rest):
        across, out = rest[:-1], rest[-1]
        across = [a[...] for a in across] if len(across) == 2 else [across[0][0], across[0][1]]
        kept = own[...] + across[0].astype(F32)
        other = beside[...].astype(F32) + across[1].astype(F32)
        mine = half[0] == 0
        out[0] = jnp.where(mine, kept, other)
        out[1] = jnp.where(mine, other, kept)

    rows = pl.BlockSpec((tile, width), lambda i, _: (i, 0))
    both = pl.BlockSpec((2, tile, width), lambda i, _: (0, i, 0))
    return pl.pallas_call(
        kernel,
        grid_spec=pltpu.PrefetchScalarGridSpec(
            num_scalar_prefetch=1,
            grid=(count // tile,),
            in_specs=[rows, rows] + ([rows, rows] if len(across) == 2 else [both]),
            out_specs=both,
        ),
        out_shape=jax.ShapeDtypeStruct((2, count, width), F32),
        compiler_params=pltpu.CompilerParams(vmem_limit_bytes=VMEM_LIMIT),
        cost_estimate=pl.CostEstimate(flops=1000, transcendentals=0, bytes_accessed=1000),
        name=name,
    )(half.astype(jnp.int32)[None], own, beside, *across)


def taken_back(base, slot, arrived, dtype, name):
    count, width = base.shape
    tile = min(256, count)

    def kernel(base, slot, arrived, out):
        slots = lax.broadcasted_iota(jnp.int32, (tile, arrived.shape[0]), 1)
        chosen = jnp.where(slot[...] == slots, 1.0, 0.0).astype(BF16)
        out[...] = (base[...].astype(F32) + product(chosen, arrived[...])).astype(dtype)

    return call(
        kernel,
        name,
        count // tile,
        [tiles(base, tile), tiles(slot, tile), whole(arrived)],
        [rows_out((count, width), dtype, tile)],
    )[0]


def waited(array):
    def kernel(array, out):
        out[...] = array[...].astype(F32)

    return pl.pallas_call(
        kernel,
        grid=(1,),
        in_specs=[pl.BlockSpec((16, 128), lambda i: (0, 0))],
        out_specs=pl.BlockSpec((16, 128), lambda i: (0, 0)),
        out_shape=jax.ShapeDtypeStruct((16, 128), F32),
        cost_estimate=pl.CostEstimate(flops=10**11, transcendentals=0, bytes_accessed=10**8),
        name="waited",
    )(array)


def after(value, *others):
    return lax.optimization_barrier((value, *others))[0]


def per_device(tokens, routes, cotangent, ln_gain, layer_norm_bias, centroid, w_in, w_out):
    groups, halves = lax.axis_size("expert"), lax.axis_size("half")
    half = lax.axis_index("half")
    experts = groups * halves
    count, width = tokens.shape
    capacity = 2 * count // experts
    arriving = experts * capacity
    units = w_in.shape[2]
    tile = min(TILE, arriving)
    targets = routes[:, 0]

    onehot = targets[:, None] == jnp.arange(experts, dtype=jnp.int32)[None, :]
    order = jnp.arange(count, dtype=jnp.int32)
    earlier = (order[:, None] >= order[None, :]).astype(BF16)
    ranks = jnp.dot(earlier, onehot.astype(BF16), preferred_element_type=F32)
    ranks = jnp.sum(jnp.where(onehot, ranks, 0.0), axis=1).astype(jnp.int32) - 1
    slot = targets * capacity + ranks
    slots = jnp.arange(arriving, dtype=jnp.int32)

    def place(values):
        chosen = (slots[:, None] == slot[None, :]).astype(BF16)
        return jnp.dot(chosen, values, preferred_element_type=F32).astype(BF16)

    def exchange(rows):
        rows = rows.reshape(experts, capacity, width)
        return lax.all_to_all(
            rows, ("expert", "half"), split_axis=0, concat_axis=0, tiled=True
        ).reshape(arriving, width)

    def over(axis, value):
        size = lax.axis_size(axis)
        return lax.ppermute(value, axis, [(i, size - 1 - i) for i in range(size)])

    def diagonal(value):
        return lax.ppermute(value, ("sub", "half"), [(i, 3 - i) for i in range(4)])

    def pick(stacked, index):
        return lax.dynamic_index_in_dim(stacked, index, 0, keepdims=False)

    gain = pick(ln_gain, half).astype(F32)[None, :]
    bias = pick(layer_norm_bias, half).astype(F32)[None, :]
    center = pick(centroid, half).astype(F32)[None, :]

    own = [pick(w_in, half), pick(w_out, half)]
    other = [over("half", pick(w, 1 - half)) for w in (w_in, w_out)]
    across = [over("sub", w) for w in own]
    ends = [0, units // 4, units * 3 // 4, units]

    def piece(number):
        start, end = ends[number : number + 2]
        return [other[0][:, start:end], other[1][start:end]]

    far = [over("sub", w) for w in piece(0)]
    x = exchange(place(tokens))
    far[1], *_ = lax.optimization_barrier((far[1], far[0], *across))
    x, dy_sent, mark, own[0], own[1], other[0], other[1], across[0], across[1], far[0], far[1] = lax.optimization_barrier(
        (x, place(cotangent), waited(far[1]), *own, *other, *across, *far)
    )
    dy = exchange(dy_sent)
    far += [over("sub", w) for w in piece(1)]
    near_weights = [*own, *other, *across]

    normed, hidden1, slope1, mixed, gates = call(
        forward_near,
        "forward_near",
        arriving // tile,
        [tiles(x, tile)] + [whole(a) for a in (gain, bias, center, *near_weights)]
        + [(mark, "out", None)],
        [
            rows_out((arriving, width), BF16, tile),
            rows_out((arriving, 3 * units), BF16, tile),
            rows_out((arriving, 3 * units), BF16, tile),
            rows_out((arriving, width), F32, tile),
            rows_out((arriving, 128), F32, tile),
        ],
    )
    normed, *far = lax.optimization_barrier((normed, *far))
    last = [over("sub", after(w, normed)) for w in piece(2)]
    some = ((arriving, units), BF16, (tile, ends[2]), lambda i: (i, 0))
    hidden2, slope2, mixed = call(
        forward_more,
        "forward_more",
        arriving // tile,
        [tiles(normed, tile), tiles(mixed, tile)] + [whole(w) for w in far],
        [some, some, rows_out((arriving, width), F32, tile)],
    )
    far += last
    some = ((arriving, units), BF16, (tile, units - ends[2]), lambda i: (i, ends[2] // (units - ends[2])))
    hidden2, slope2, gated = call(
        forward_last,
        "forward_last",
        arriving // tile,
        [tiles(normed, tile), tiles(mixed, tile), tiles(gates, tile)]
        + [whole(w) for w in last]
        + [(hidden2, "out", None), (slope2, "out", None)],
        [some, some, rows_out((arriving, width), BF16, tile)],
        input_output_aliases={5: 0, 6: 1},
    )
    gated, dy = lax.optimization_barrier((gated, dy))
    returned = exchange(gated)

    def block_in(near, far, number):
        return (near, number) if number < 3 else (far, number - 3)

    def out_part(number, dtype):
        left = block_in(hidden1, hidden2, number)
        return weight_grad(left, (mixed_grad, 0), units, width, dtype, "out_weight_grad")

    def in_part(number, dtype, beside=None, apart=False):
        right = block_in(grad1, grad2, number)
        return weight_grad((normed, 0), right, width, units, dtype, "in_weight_grad", beside, apart)

    out_sent, mixed_grad = first_weight_grad(hidden2, dy, gates, units, "out_weight_grad")
    out_sent = [out_part(2, BF16), out_sent]
    out_across = [over("sub", out_sent[0]), diagonal(out_sent[1])]
    grad1, grad2, expert_grad, sums = call(
        backward,
        "backward",
        arriving // tile,
        [tiles(a, tile) for a in (x, after(dy, *out_sent), gated, slope1, slope2, gates)]
        + [whole(a) for a in (gain, center, *near_weights, *far)],
        [
            rows_out((arriving, 3 * units), BF16, tile),
            rows_out((arriving, units), BF16, tile),
            rows_out((arriving, width), BF16, tile),
            ((8, width), F32, (8, width), lambda i: (0, 0)),
        ],
    )
    in_sent = [over("half", p) for p in in_part(3, BF16, apart=True)]
    out_sent = out_part(1, BF16)
    normed, out_sent = lax.optimization_barrier((normed, out_sent))
    in_across = in_part(2, BF16, in_sent)
    moved = [over("sub", sums), over("half", sums), diagonal(sums)]
    expert_grad, returned, in_across, *moved = lax.optimization_barrier(
        (expert_grad, returned, in_across, *out_across, *moved)
    )
    out_across, moved = moved[:2], moved[2:]
    back = exchange(expert_grad)
    in_across = over("sub", in_across)
    out_beside, in_beside = over("half", out_sent), over("half", in_part(1, BF16))
    layer_out = taken_back(tokens, slot[:, None], returned, BF16, "layer_out")
    out_wgrad = joined(half, out_part(0, F32), out_beside, out_across, "out_weight_grad_joined")
    in_own, layer_out, out_wgrad = lax.optimization_barrier((in_part(0, F32), layer_out, out_wgrad))
    in_wgrad = joined(half, in_own, in_beside, [in_across], "in_weight_grad_joined")
    kept, other_sums = sums + moved[0], moved[1] + moved[2]
    small = jnp.where((jnp.arange(halves) == half)[:, None, None], kept[None], other_sums[None])
    tokens_grad = taken_back(cotangent, slot[:, None], back, F32, "tokens_grad")
    return (layer_out, tokens_grad, small[:, 0], small[:, 1], small[:, 2], in_wgrad, out_wgrad)


def solution(mesh):
    groups, tensor = mesh.shape["expert"], mesh.shape["tensor"]
    halves = 2
    split = Mesh(
        mesh.devices.reshape(groups, tensor // halves, halves), ("expert", "sub", "half")
    )
    rows, within = P(("expert", "sub", "half"), None), P("expert", None)
    columns = P("expert", None, ("sub", "half"))
    depth = P("expert", ("sub", "half"), None)
    return jax.shard_map(
        per_device,
        mesh=split,
        in_specs=(rows, rows, rows, within, within, within, columns, depth),
        out_specs=(rows, rows, within, within, within, columns, depth),
        check_vma=False,
    )
```

```python
import functools

import jax
import jax.numpy as jnp
from jax import lax
from jax.experimental import pallas as pl
from jax.experimental.pallas import tpu as pltpu
from jax.sharding import Mesh
from jax.sharding import PartitionSpec as P

epsilon = 1e-05
F32 = jnp.float32
BF16 = jnp.bfloat16
LAST = (((1,), (1,)), ((), ()))
ROWS = (((0,), (0,)), ((), ()))
VMEM_LIMIT = 58 * 2**20
TILE = 512


def product(a, b, dims=(((1,), (0,)), ((), ()))):
    return lax.dot_general(a, b, dims, preferred_element_type=F32)


def standardize(x):
    centered = x - jnp.mean(x, axis=-1, keepdims=True)
    inverse = lax.rsqrt(jnp.mean(centered * centered, axis=-1, keepdims=True) + epsilon)
    return centered * inverse, inverse


def steps_of(weights):
    for first, second in weights:
        step = min(TILE, first.shape[1]) if first.shape[1] % TILE == 0 else first.shape[1]
        for start in range(0, first.shape[1], step):
            yield first[:, start : start + step], second[start : start + step, :]


def through(normed, weights, hidden_ref, slope_ref):
    total, at = None, 0
    for first, second in steps_of(weights):
        z = product(normed, first)
        cumul = 0.5 * (1.0 + lax.erf(z * 0.7071067811865476))
        density = jnp.exp(-0.5 * z * z) * 0.3989422804014327
        hidden = (z * cumul).astype(BF16)
        hidden_ref[:, at : at + z.shape[1]] = hidden
        slope_ref[:, at : at + z.shape[1]] = (cumul + z * density).astype(BF16)
        part = product(hidden, second)
        total = part if total is None else total + part
        at += z.shape[1]
    return total


def paired(refs):
    return list(zip(refs[::2], refs[1::2]))


def forward_near(x, gain, bias, center, *rest):
    weights, (normed, hidden, slope, mixed, gates) = paired(rest[:-6]), rest[-5:]
    values = x[...].astype(F32)
    rows = (standardize(values)[0] * gain[...] + bias[...]).astype(BF16)
    normed[...] = rows
    mixed[...] = through(rows, weights, hidden, slope)
    gate = jax.nn.sigmoid(jnp.sum(values * center[...], axis=-1, keepdims=True))
    gates[...] = jnp.broadcast_to(gate, gates.shape)


def forward_more(rows, near, *rest):
    weights, (hidden, slope, mixed) = paired(rest[:-3]), rest[-3:]
    mixed[...] = near[...] + through(rows[...], weights, hidden, slope)


def forward_last(rows, near, gates, first, second, kept_hidden, kept_slope, hidden, slope, gated):
    del kept_hidden, kept_slope
    whole = near[...] + through(rows[...], [(first, second)], hidden, slope)
    gated[...] = (gates[:, :1] * whole).astype(BF16)


def backward(ends, x, dy, gated, s1, s2, gates, gain, center, *rest):
    count = 6 + 2 * (len(ends) - 1)
    refs, (g1, g2, expert_grad, sums), (ins, outs, sems) = rest[:count], rest[count:-3], rest[-3:]
    units = outs.shape[0] // 4
    step = min(TILE, units)
    copies = []
    for number, (first, second) in enumerate(paired(refs)):
        columns = pl.ds(number * units if number < 3 else 3 * units + ends[number - 3], first.shape[1])
        copies += [
            (min(number, 3), pltpu.make_async_copy(second, outs.at[columns, :], sems.at[2 * number])),
            (4, pltpu.make_async_copy(first, ins.at[:, columns], sems.at[2 * number + 1])),
        ]
    copies.sort(key=lambda c: c[0])

    @pl.when(pl.program_id(0) == 0)
    def _():
        for _, copy in copies:
            copy.start()
        sums[...] = jnp.zeros_like(sums)

    rows = x[...].astype(F32)
    gate = gates[:, :1]
    upper = dy[...].astype(F32)
    mixed_grad = (gate * upper).astype(BF16)
    for block in range(5):

        @pl.when(pl.program_id(0) == 0)
        def _():
            for used, copy in copies:
                if used == block:
                    copy.wait()

        for at in range(block * units, min(block + 1, 4) * units, step):
            hidden_grad = product(mixed_grad, outs[at : at + step, :], LAST)
            slope, grad, at = (s1, g1, at) if block < 3 else (s2, g2, at - 3 * units)
            grad[:, at : at + step] = (hidden_grad * slope[:, at : at + step].astype(F32)).astype(BF16)
    total = product(g1[...], ins[:, : 3 * units], LAST) + product(g2[...], ins[:, 3 * units :], LAST)
    xhat, inverse = standardize(rows)
    logit_grad = jnp.sum(upper * gated[...].astype(F32), axis=-1, keepdims=True) * (1.0 - gate)
    u = total * gain[...]
    expert_grad[...] = (
        inverse
        * (u - jnp.mean(u, axis=-1, keepdims=True) - xhat * jnp.mean(u * xhat, axis=-1, keepdims=True))
        + logit_grad * center[...]
    ).astype(BF16)
    sums[0:1, :] += jnp.sum(total * xhat, axis=0, keepdims=True)
    sums[1:2, :] += jnp.sum(total, axis=0, keepdims=True)
    sums[2:3, :] += jnp.sum(logit_grad * rows, axis=0, keepdims=True)


def call(kernel, name, steps, ins, outs, **more):
    def spec(shape, block, index):
        if block == "out":
            return pl.BlockSpec(memory_space=pl.ANY)
        if block is None:
            return pl.BlockSpec(shape, lambda *_: (0,) * len(shape), pipeline_mode=pl.Buffered(1))
        return pl.BlockSpec(block, index)

    return pl.pallas_call(
        kernel,
        grid=(steps,),
        in_specs=[spec(a.shape, block, index) for a, block, index in ins],
        out_specs=[pl.BlockSpec(block, index) for _, _, block, index in outs],
        out_shape=[jax.ShapeDtypeStruct(shape, dtype) for shape, dtype, _, _ in outs],
        compiler_params=pltpu.CompilerParams(vmem_limit_bytes=VMEM_LIMIT),
        cost_estimate=pl.CostEstimate(flops=1000, transcendentals=0, bytes_accessed=1000),
        name=name,
        **more,
    )(*[a for a, _, _ in ins])


def tiles(array, tile):
    return array, (tile, array.shape[1]), lambda i: (i, 0)


def rows_out(shape, dtype, tile):
    return shape, dtype, (tile, shape[1]), lambda i: (i, 0)


def whole(array):
    return array, None, None


def weight_grad(left, right, units, width, dtype, name, apart=False):
    (a, i), (b, j) = left, right
    tile = min(TILE, units)
    steps = units // tile

    def kernel(a, b, *outs):
        total = product(a[...], b[...], ROWS).astype(dtype)
        if not apart:
            outs[0][...] = total
        for n in range(steps if apart else 0):

            @pl.when(pl.program_id(0) == n)
            def _():
                outs[n][...] = total

    ins = [
        (a, (a.shape[0], tile), lambda n: (0, i * steps + n)),
        (b, (b.shape[0], width), lambda n: (0, j)),
    ]
    if apart:
        return call(kernel, name, steps, ins, [((tile, width), dtype, (tile, width), lambda n: (0, 0))] * steps)
    return call(kernel, name, steps, ins, [rows_out((units, width), dtype, tile)])[0]


def first_weight_grad(hidden, dy, gates, units, name):
    count, width = dy.shape
    tile = min(TILE, units)

    def kernel(a, dy, gates, out, mixed_grad):
        @pl.when(pl.program_id(0) == 0)
        def _():
            mixed_grad[...] = (gates[:, :1] * dy[...].astype(F32)).astype(BF16)

        out[...] = product(a[...], mixed_grad[...], ROWS).astype(BF16)

    return call(
        kernel,
        name,
        units // tile,
        [(hidden, (count, tile), lambda n: (0, n)), whole(dy), whole(gates)],
        [rows_out((units, width), BF16, tile), ((count, width), BF16, (count, width), lambda n: (0, 0))],
    )


def sums_into(number, operands, held, name):
    count, width = operands[0].shape
    tile = min(256, count)
    flat, ends = [], []
    for o in operands:
        pieces = o if isinstance(o, list) else [o]
        at = 0
        for p in pieces:
            flat.append(p)
            ends.append((at, at + p.shape[0] // tile))
            at += p.shape[0] // tile

    def kernel(number, *refs):
        out = refs[-1]
        step, total = pl.program_id(0), None
        for ref, (start, end) in zip(refs, ends):
            part = ref[...].astype(F32)
            if (start, end) != (0, count // tile):
                part = jnp.where((step >= start) & (step < end), part, 0.0)
            total = part if total is None else total + part
        out[0] = total

    def rows(start, end):
        return pl.BlockSpec((tile, width), lambda i, _: (jnp.clip(i - start, 0, end - start - 1), 0))

    extra = [] if held is None else [held]
    return pl.pallas_call(
        kernel,
        grid_spec=pltpu.PrefetchScalarGridSpec(
            num_scalar_prefetch=1,
            grid=(count // tile,),
            in_specs=[rows(*e) for e in ends] + [pl.BlockSpec(memory_space=pl.ANY)] * len(extra),
            out_specs=pl.BlockSpec((1, tile, width), lambda i, number: (number[0], i, 0)),
        ),
        out_shape=jax.ShapeDtypeStruct((2, count, width), F32),
        input_output_aliases={1 + len(flat): 0} if extra else {},
        compiler_params=pltpu.CompilerParams(vmem_limit_bytes=VMEM_LIMIT),
        cost_estimate=pl.CostEstimate(flops=1000, transcendentals=0, bytes_accessed=1000),
        name=name,
    )(number.astype(jnp.int32)[None], *flat, *extra)


def taken_back(base, slot, arrived, dtype, name):
    count, width = base.shape
    tile = min(512, count)

    def kernel(base, slot, arrived, out):
        slots = lax.broadcasted_iota(jnp.int32, (tile, arrived.shape[0]), 1)
        chosen = jnp.where(slot[...] == slots, 1.0, 0.0).astype(BF16)
        out[...] = (base[...].astype(F32) + product(chosen, arrived[...])).astype(dtype)

    return call(
        kernel,
        name,
        count // tile,
        [tiles(base, tile), tiles(slot, tile), whole(arrived)],
        [rows_out((count, width), dtype, tile)],
    )[0]


def waited(array):
    def kernel(array, out):
        out[...] = array[...].astype(F32)

    return pl.pallas_call(
        kernel,
        grid=(1,),
        in_specs=[pl.BlockSpec((16, 128), lambda i: (0, 0))],
        out_specs=pl.BlockSpec((16, 128), lambda i: (0, 0)),
        out_shape=jax.ShapeDtypeStruct((16, 128), F32),
        cost_estimate=pl.CostEstimate(flops=10**11, transcendentals=0, bytes_accessed=10**8),
        name="waited",
    )(array)


def after(value, *others):
    return lax.optimization_barrier((value, *others))[0]


def per_device(tokens, routes, cotangent, ln_gain, layer_norm_bias, centroid, w_in, w_out):
    groups, halves = lax.axis_size("expert"), lax.axis_size("half")
    half = lax.axis_index("half")
    experts = groups * halves
    count, width = tokens.shape
    capacity = 2 * count // experts
    arriving = experts * capacity
    units = w_in.shape[2]
    tile = min(TILE, arriving)
    targets = routes[:, 0]

    onehot = targets[:, None] == jnp.arange(experts, dtype=jnp.int32)[None, :]
    order = jnp.arange(count, dtype=jnp.int32)
    earlier = (order[:, None] >= order[None, :]).astype(BF16)
    ranks = jnp.dot(earlier, onehot.astype(BF16), preferred_element_type=F32)
    ranks = jnp.sum(jnp.where(onehot, ranks, 0.0), axis=1).astype(jnp.int32) - 1
    slot = targets * capacity + ranks
    slots = jnp.arange(arriving, dtype=jnp.int32)

    def place(values):
        chosen = (slots[:, None] == slot[None, :]).astype(BF16)
        return jnp.dot(chosen, values, preferred_element_type=F32).astype(BF16)

    def exchange(rows):
        rows = rows.reshape(experts, capacity, width)
        return lax.all_to_all(
            rows, ("expert", "half"), split_axis=0, concat_axis=0, tiled=True
        ).reshape(arriving, width)

    def over(axis, value):
        size = lax.axis_size(axis)
        return lax.ppermute(value, axis, [(i, size - 1 - i) for i in range(size)])

    def diagonal(value):
        return lax.ppermute(value, ("sub", "half"), [(i, 3 - i) for i in range(4)])

    def pick(stacked, index):
        return lax.dynamic_index_in_dim(stacked, index, 0, keepdims=False)

    gain = pick(ln_gain, half).astype(F32)[None, :]
    bias = pick(layer_norm_bias, half).astype(F32)[None, :]
    center = pick(centroid, half).astype(F32)[None, :]

    own = [pick(w_in, half), pick(w_out, half)]
    other = [pick(over("half", w), half) for w in (w_in, w_out)]
    across = [over("sub", w) for w in own]
    ends = [0, units // 8, units * 3 // 4, units]

    def piece(number):
        start, end = ends[number : number + 2]
        first = lax.dynamic_slice(w_in, (1 - half, 0, start), (1, width, end - start))
        return [first[0], lax.dynamic_slice(w_out, (1 - half, start, 0), (1, end - start, width))[0]]

    mark = waited(across[0])
    far = [diagonal(after(w, mark)) for w in piece(0)]
    x = exchange(place(tokens))
    sent = [*piece(1), *piece(2)]
    x, dy_sent, mark, *arrived = lax.optimization_barrier(
        (x, place(cotangent), mark, *own, *other, *across, *far, *sent)
    )
    own, other, across, far, sent = (arrived[n : n + 2] for n in (0, 2, 4, 6, 8))
    later = arrived[10:]
    dy = exchange(dy_sent)
    far = list(far) + [diagonal(w) for w in sent]
    near_weights = [*own, *other, *across]

    normed, hidden1, slope1, mixed, gates = call(
        forward_near,
        "forward_near",
        arriving // tile,
        [tiles(x, tile)] + [whole(a) for a in (gain, bias, center, *near_weights)]
        + [(mark, "out", None)],
        [
            rows_out((arriving, width), BF16, tile),
            rows_out((arriving, 3 * units), BF16, tile),
            rows_out((arriving, 3 * units), BF16, tile),
            rows_out((arriving, width), F32, tile),
            rows_out((arriving, 128), F32, tile),
        ],
    )
    normed, *far = lax.optimization_barrier((normed, *far))
    last = [diagonal(after(w, normed)) for w in later]
    some = ((arriving, units), BF16, (tile, ends[2]), lambda i: (i, 0))
    hidden2, slope2, mixed = call(
        forward_more,
        "forward_more",
        arriving // tile,
        [tiles(normed, tile), tiles(mixed, tile)] + [whole(w) for w in far],
        [some, some, rows_out((arriving, width), F32, tile)],
    )
    far += last
    some = ((arriving, units), BF16, (tile, units - ends[2]), lambda i: (i, ends[2] // (units - ends[2])))
    hidden2, slope2, gated = call(
        forward_last,
        "forward_last",
        arriving // tile,
        [tiles(normed, tile), tiles(mixed, tile), tiles(gates, tile)]
        + [whole(w) for w in last]
        + [(hidden2, "out", None), (slope2, "out", None)],
        [some, some, rows_out((arriving, width), BF16, tile)],
        input_output_aliases={5: 0, 6: 1},
    )
    gated, dy = lax.optimization_barrier((gated, dy))
    returned = exchange(gated)

    def block_in(near, far, number):
        return (near, number) if number < 3 else (far, number - 3)

    def out_part(number, dtype):
        left = block_in(hidden1, hidden2, number)
        return weight_grad(left, (mixed_grad, 0), units, width, dtype, "out_weight_grad")

    def in_part(number, dtype, apart=False):
        right = block_in(grad1, grad2, number)
        return weight_grad((normed, 0), right, width, units, dtype, "in_weight_grad", apart)

    out_sent, mixed_grad = first_weight_grad(hidden2, dy, gates, units, "out_weight_grad")
    out_sent = [out_part(2, BF16), out_sent]
    out_across = [over("sub", out_sent[0]), diagonal(out_sent[1])]
    grad1, grad2, expert_grad, sums = call(
        functools.partial(backward, ends),
        "backward",
        arriving // tile,
        [tiles(a, tile) for a in (x, after(dy, *out_sent), gated, slope1, slope2, gates)]
        + [whole(a) for a in (gain, center)]
        + [(a, "out", None) for a in (*near_weights, *far)],
        [
            rows_out((arriving, 3 * units), BF16, tile),
            rows_out((arriving, units), BF16, tile),
            rows_out((arriving, width), BF16, tile),
            ((8, width), F32, (8, width), lambda i: (0, 0)),
        ],
        scratch_shapes=[
            pltpu.VMEM((width, 4 * units), BF16),
            pltpu.VMEM((4 * units, width), BF16),
            pltpu.SemaphoreType.DMA((12,)),
        ],
    )
    grad2, out_across[1] = lax.optimization_barrier((grad2, out_across[1]))
    in_sent = [in_part(3, BF16), in_part(2, BF16)]
    out_sent = out_part(1, BF16)
    moved = [over("sub", sums), over("half", sums), diagonal(sums)]
    expert_grad, returned, hidden1, in_sent[0], in_sent[1], out_sent, *moved = lax.optimization_barrier(
        (expert_grad, returned, hidden1, *in_sent, out_sent, *out_across, *moved)
    )
    out_across, moved = moved[:2], moved[2:]
    back = exchange(expert_grad)
    in_across = [over("sub", in_sent[1]), diagonal(in_sent[0])]
    out_beside = over("half", out_sent)
    in_beside = [over("half", p) for p in in_part(1, BF16, apart=True)]
    layer_out = taken_back(tokens, slot[:, None], returned, BF16, "layer_out")
    out_wgrad = sums_into(1 - half, [out_across[1], out_beside], None, "out_weight_grad_other")
    out_wgrad = sums_into(half, [out_part(0, F32), out_across[0]], out_wgrad, "out_weight_grad_own")
    in_own, layer_out, out_wgrad = lax.optimization_barrier((in_part(0, F32), layer_out, out_wgrad))
    in_wgrad = sums_into(1 - half, [in_across[1], in_beside], None, "in_weight_grad_other")
    in_wgrad = sums_into(half, [in_own, in_across[0]], in_wgrad, "in_weight_grad_own")
    kept, other_sums = sums + moved[0], moved[1] + moved[2]
    small = jnp.where((jnp.arange(halves) == half)[:, None, None], kept[None], other_sums[None])
    tokens_grad = taken_back(cotangent, slot[:, None], back, F32, "tokens_grad")
    return (layer_out, tokens_grad, small[:, 0], small[:, 1], small[:, 2], in_wgrad, out_wgrad)


def solution(mesh):
    groups, tensor = mesh.shape["expert"], mesh.shape["tensor"]
    halves = 2
    split = Mesh(
        mesh.devices.reshape(groups, tensor // halves, halves), ("expert", "sub", "half")
    )
    rows, within = P(("expert", "sub", "half"), None), P("expert", None)
    columns = P("expert", None, ("sub", "half"))
    depth = P("expert", ("sub", "half"), None)
    return jax.shard_map(
        per_device,
        mesh=split,
        in_specs=(rows, rows, rows, within, within, within, columns, depth),
        out_specs=(rows, rows, within, within, within, columns, depth),
        check_vma=False,
    )
```

```python
import functools

import jax
import jax.numpy as jnp
from jax import lax
from jax.experimental import pallas as pl
from jax.experimental.pallas import tpu as pltpu
from jax.sharding import Mesh
from jax.sharding import PartitionSpec as P

epsilon = 1e-05
F32 = jnp.float32
BF16 = jnp.bfloat16
LAST = (((1,), (1,)), ((), ()))
ROWS = (((0,), (0,)), ((), ()))
VMEM_LIMIT = 58 * 2**20
TILE = 512


def product(a, b, dims=(((1,), (0,)), ((), ()))):
    return lax.dot_general(a, b, dims, preferred_element_type=F32)


def standardize(x):
    centered = x - jnp.mean(x, axis=-1, keepdims=True)
    inverse = lax.rsqrt(jnp.mean(centered * centered, axis=-1, keepdims=True) + epsilon)
    return centered * inverse, inverse


def steps_of(weights):
    for first, second in weights:
        step = min(TILE, first.shape[1]) if first.shape[1] % TILE == 0 else first.shape[1]
        for start in range(0, first.shape[1], step):
            yield first[:, start : start + step], second[start : start + step, :]


def through(normed, weights, hidden_ref, slope_ref):
    total, at = None, 0
    for first, second in steps_of(weights):
        z = product(normed, first)
        cumul = 0.5 * (1.0 + lax.erf(z * 0.7071067811865476))
        density = jnp.exp(-0.5 * z * z) * 0.3989422804014327
        hidden = (z * cumul).astype(BF16)
        hidden_ref[:, at : at + z.shape[1]] = hidden
        slope_ref[:, at : at + z.shape[1]] = (cumul + z * density).astype(BF16)
        part = product(hidden, second)
        total = part if total is None else total + part
        at += z.shape[1]
    return total


def paired(refs):
    return list(zip(refs[::2], refs[1::2]))


def forward_near(x, gain, bias, center, *rest):
    weights, (normed, hidden, slope, mixed, gates) = paired(rest[:-6]), rest[-5:]
    values = x[...].astype(F32)
    rows = (standardize(values)[0] * gain[...] + bias[...]).astype(BF16)
    normed[...] = rows
    mixed[...] = through(rows, weights, hidden, slope)
    gate = jax.nn.sigmoid(jnp.sum(values * center[...], axis=-1, keepdims=True))
    gates[...] = jnp.broadcast_to(gate, gates.shape)


def forward_more(rows, near, *rest):
    weights, (hidden, slope, mixed) = paired(rest[:-3]), rest[-3:]
    mixed[...] = near[...] + through(rows[...], weights, hidden, slope)


def forward_last(rows, near, gates, first, second, kept_hidden, kept_slope, hidden, slope, gated):
    del kept_hidden, kept_slope
    whole = near[...] + through(rows[...], [(first, second)], hidden, slope)
    gated[...] = (gates[:, :1] * whole).astype(BF16)


def backward(ends, x, dy, gated, s1, s2, gates, gain, center, *rest):
    count = 6 + 2 * (len(ends) - 1)
    refs, (g1, g2, expert_grad, sums), (ins, outs, sems) = rest[:count], rest[count:-3], rest[-3:]
    units = outs.shape[0] // 4
    step = min(TILE, units)
    copies = []
    for number, (first, second) in enumerate(paired(refs)):
        columns = pl.ds(number * units if number < 3 else 3 * units + ends[number - 3], first.shape[1])
        copies += [
            (min(number, 3), pltpu.make_async_copy(second, outs.at[columns, :], sems.at[2 * number])),
            (4, pltpu.make_async_copy(first, ins.at[:, columns], sems.at[2 * number + 1])),
        ]
    copies.sort(key=lambda c: c[0])

    @pl.when(pl.program_id(0) == 0)
    def _():
        for _, copy in copies:
            copy.start()
        sums[...] = jnp.zeros_like(sums)

    rows = x[...].astype(F32)
    gate = gates[:, :1]
    upper = dy[...].astype(F32)
    mixed_grad = (gate * upper).astype(BF16)
    for block in range(5):

        @pl.when(pl.program_id(0) == 0)
        def _():
            for used, copy in copies:
                if used == block:
                    copy.wait()

        for at in range(block * units, min(block + 1, 4) * units, step):
            hidden_grad = product(mixed_grad, outs[at : at + step, :], LAST)
            slope, grad, at = (s1, g1, at) if block < 3 else (s2, g2, at - 3 * units)
            grad[:, at : at + step] = (hidden_grad * slope[:, at : at + step].astype(F32)).astype(BF16)
    total = product(g1[...], ins[:, : 3 * units], LAST) + product(g2[...], ins[:, 3 * units :], LAST)
    xhat, inverse = standardize(rows)
    logit_grad = jnp.sum(upper * gated[...].astype(F32), axis=-1, keepdims=True) * (1.0 - gate)
    u = total * gain[...]
    expert_grad[...] = (
        inverse
        * (u - jnp.mean(u, axis=-1, keepdims=True) - xhat * jnp.mean(u * xhat, axis=-1, keepdims=True))
        + logit_grad * center[...]
    ).astype(BF16)
    sums[0:1, :] += jnp.sum(total * xhat, axis=0, keepdims=True)
    sums[1:2, :] += jnp.sum(total, axis=0, keepdims=True)
    sums[2:3, :] += jnp.sum(logit_grad * rows, axis=0, keepdims=True)


def call(kernel, name, steps, ins, outs, **more):
    def spec(shape, block, index):
        if block == "out":
            return pl.BlockSpec(memory_space=pl.ANY)
        if block is None:
            return pl.BlockSpec(shape, lambda *_: (0,) * len(shape), pipeline_mode=pl.Buffered(1))
        return pl.BlockSpec(block, index)

    return pl.pallas_call(
        kernel,
        grid=(steps,),
        in_specs=[spec(a.shape, block, index) for a, block, index in ins],
        out_specs=[pl.BlockSpec(block, index) for _, _, block, index in outs],
        out_shape=[jax.ShapeDtypeStruct(shape, dtype) for shape, dtype, _, _ in outs],
        compiler_params=pltpu.CompilerParams(vmem_limit_bytes=VMEM_LIMIT),
        cost_estimate=pl.CostEstimate(flops=1000, transcendentals=0, bytes_accessed=1000),
        name=name,
        **more,
    )(*[a for a, _, _ in ins])


def tiles(array, tile):
    return array, (tile, array.shape[1]), lambda i: (i, 0)


def rows_out(shape, dtype, tile):
    return shape, dtype, (tile, shape[1]), lambda i: (i, 0)


def whole(array):
    return array, None, None


def weight_grad(left, right, units, width, dtype, name, apart=False):
    (a, i), (b, j) = left, right
    tile = min(TILE, units)
    steps = units // tile

    def kernel(a, b, *outs):
        total = product(a[...], b[...], ROWS).astype(dtype)
        if not apart:
            outs[0][...] = total
        for n in range(steps if apart else 0):

            @pl.when(pl.program_id(0) == n)
            def _():
                outs[n][...] = total

    ins = [
        (a, (a.shape[0], tile), lambda n: (0, i * steps + n)),
        (b, (b.shape[0], width), lambda n: (0, j)),
    ]
    if apart:
        return call(kernel, name, steps, ins, [((tile, width), dtype, (tile, width), lambda n: (0, 0))] * steps)
    return call(kernel, name, steps, ins, [rows_out((units, width), dtype, tile)])[0]


def first_weight_grad(hidden, dy, gates, units, name):
    count, width = dy.shape
    tile = min(TILE, units)

    def kernel(a, dy, gates, out, mixed_grad):
        @pl.when(pl.program_id(0) == 0)
        def _():
            mixed_grad[...] = (gates[:, :1] * dy[...].astype(F32)).astype(BF16)

        out[...] = product(a[...], mixed_grad[...], ROWS).astype(BF16)

    return call(
        kernel,
        name,
        units // tile,
        [(hidden, (count, tile), lambda n: (0, n)), whole(dy), whole(gates)],
        [rows_out((units, width), BF16, tile), ((count, width), BF16, (count, width), lambda n: (0, 0))],
    )


def sums_into(number, operands, held, name):
    count, width = operands[0].shape
    tile = min(256, count)
    flat, ends = [], []
    for o in operands:
        pieces = o if isinstance(o, list) else [o]
        at = 0
        for p in pieces:
            flat.append(p)
            ends.append((at, at + p.shape[0] // tile))
            at += p.shape[0] // tile

    def kernel(number, *refs):
        out = refs[-1]
        step, total = pl.program_id(0), None
        for ref, (start, end) in zip(refs, ends):
            part = ref[...].astype(F32)
            if (start, end) != (0, count // tile):
                part = jnp.where((step >= start) & (step < end), part, 0.0)
            total = part if total is None else total + part
        out[0] = total

    def rows(start, end):
        return pl.BlockSpec((tile, width), lambda i, _: (jnp.clip(i - start, 0, end - start - 1), 0))

    extra = [] if held is None else [held]
    return pl.pallas_call(
        kernel,
        grid_spec=pltpu.PrefetchScalarGridSpec(
            num_scalar_prefetch=1,
            grid=(count // tile,),
            in_specs=[rows(*e) for e in ends] + [pl.BlockSpec(memory_space=pl.ANY)] * len(extra),
            out_specs=pl.BlockSpec((1, tile, width), lambda i, number: (number[0], i, 0)),
        ),
        out_shape=jax.ShapeDtypeStruct((2, count, width), F32),
        input_output_aliases={1 + len(flat): 0} if extra else {},
        compiler_params=pltpu.CompilerParams(vmem_limit_bytes=VMEM_LIMIT),
        cost_estimate=pl.CostEstimate(flops=1000, transcendentals=0, bytes_accessed=1000),
        name=name,
    )(number.astype(jnp.int32)[None], *flat, *extra)


def taken_back(base, slot, arrived, dtype, name):
    count, width = base.shape
    tile = min(512, count)

    def kernel(base, slot, arrived, out):
        slots = lax.broadcasted_iota(jnp.int32, (tile, arrived.shape[0]), 1)
        chosen = jnp.where(slot[...] == slots, 1.0, 0.0).astype(BF16)
        out[...] = (base[...].astype(F32) + product(chosen, arrived[...])).astype(dtype)

    return call(
        kernel,
        name,
        count // tile,
        [tiles(base, tile), tiles(slot, tile), whole(arrived)],
        [rows_out((count, width), dtype, tile)],
    )[0]


def finish(number, own, across, held, base, slot, arrived, steps=2):
    count, width = own.shape
    tile, tokens = count // steps, base.shape[0] // steps

    def kernel(number, own, across, base, slot, arrived, held, grad, out):
        slots = lax.broadcasted_iota(jnp.int32, (tokens, arrived.shape[0]), 1)
        chosen = jnp.where(slot[...] == slots, 1.0, 0.0).astype(BF16)
        out[...] = base[...].astype(F32) + product(chosen, arrived[...])
        grad[0] = own[...] + across[...].astype(F32)

    def rows(tile, width):
        return pl.BlockSpec((tile, width), lambda i, _: (i, 0))

    return pl.pallas_call(
        kernel,
        grid_spec=pltpu.PrefetchScalarGridSpec(
            num_scalar_prefetch=1,
            grid=(steps,),
            in_specs=[
                rows(tile, width),
                rows(tile, width),
                rows(tokens, base.shape[1]),
                rows(tokens, 1),
                pl.BlockSpec(arrived.shape, lambda i, _: (0, 0), pipeline_mode=pl.Buffered(1)),
                pl.BlockSpec(memory_space=pl.ANY),
            ],
            out_specs=[
                pl.BlockSpec((1, tile, width), lambda i, number: (number[0], i, 0)),
                rows(tokens, base.shape[1]),
            ],
        ),
        out_shape=[jax.ShapeDtypeStruct(held.shape, F32), jax.ShapeDtypeStruct(base.shape, F32)],
        input_output_aliases={6: 0},
        compiler_params=pltpu.CompilerParams(vmem_limit_bytes=VMEM_LIMIT),
        cost_estimate=pl.CostEstimate(flops=1000, transcendentals=0, bytes_accessed=1000),
        name="in_weight_grad_own_and_tokens_grad",
    )(number.astype(jnp.int32)[None], own, across, base, slot, arrived, held)


def waited(array):
    def kernel(array, out):
        out[...] = array[...].astype(F32)

    return pl.pallas_call(
        kernel,
        grid=(1,),
        in_specs=[pl.BlockSpec((16, 128), lambda i: (0, 0))],
        out_specs=pl.BlockSpec((16, 128), lambda i: (0, 0)),
        out_shape=jax.ShapeDtypeStruct((16, 128), F32),
        cost_estimate=pl.CostEstimate(flops=10**11, transcendentals=0, bytes_accessed=10**8),
        name="waited",
    )(array)


def after(value, *others):
    return lax.optimization_barrier((value, *others))[0]


def per_device(tokens, routes, cotangent, ln_gain, layer_norm_bias, centroid, w_in, w_out):
    groups, halves = lax.axis_size("expert"), lax.axis_size("half")
    half = lax.axis_index("half")
    experts = groups * halves
    count, width = tokens.shape
    capacity = 2 * count // experts
    arriving = experts * capacity
    units = w_in.shape[2]
    tile = min(TILE, arriving)
    targets = routes[:, 0]

    onehot = targets[:, None] == jnp.arange(experts, dtype=jnp.int32)[None, :]
    order = jnp.arange(count, dtype=jnp.int32)
    earlier = (order[:, None] >= order[None, :]).astype(BF16)
    ranks = jnp.dot(earlier, onehot.astype(BF16), preferred_element_type=F32)
    ranks = jnp.sum(jnp.where(onehot, ranks, 0.0), axis=1).astype(jnp.int32) - 1
    slot = targets * capacity + ranks
    slots = jnp.arange(arriving, dtype=jnp.int32)

    def place(values):
        chosen = (slots[:, None] == slot[None, :]).astype(BF16)
        return jnp.dot(chosen, values, preferred_element_type=F32).astype(BF16)

    def exchange(rows):
        rows = rows.reshape(experts, capacity, width)
        return lax.all_to_all(
            rows, ("expert", "half"), split_axis=0, concat_axis=0, tiled=True
        ).reshape(arriving, width)

    def over(axis, value):
        size = lax.axis_size(axis)
        return lax.ppermute(value, axis, [(i, size - 1 - i) for i in range(size)])

    def diagonal(value):
        return lax.ppermute(value, ("sub", "half"), [(i, 3 - i) for i in range(4)])

    def pick(stacked, index):
        return lax.dynamic_index_in_dim(stacked, index, 0, keepdims=False)

    gain = pick(ln_gain, half).astype(F32)[None, :]
    bias = pick(layer_norm_bias, half).astype(F32)[None, :]
    center = pick(centroid, half).astype(F32)[None, :]

    own = [pick(w_in, half), pick(w_out, half)]
    other = [pick(over("half", w), half) for w in (w_in, w_out)]
    across = [over("sub", w) for w in own]
    ends = [0, units // 8, units * 3 // 4, units]

    def piece(number):
        start, end = ends[number : number + 2]
        first = lax.dynamic_slice(w_in, (1 - half, 0, start), (1, width, end - start))
        return [first[0], lax.dynamic_slice(w_out, (1 - half, start, 0), (1, end - start, width))[0]]

    mark = waited(across[0])
    far = [diagonal(after(w, mark)) for w in piece(0)]
    x = exchange(place(tokens))
    sent = [*piece(1), *piece(2)]
    x, dy_sent, mark, *arrived = lax.optimization_barrier(
        (x, place(cotangent), mark, *own, *other, *across, *far, *sent)
    )
    own, other, across, far, sent = (arrived[n : n + 2] for n in (0, 2, 4, 6, 8))
    later = arrived[10:]
    dy = exchange(dy_sent)
    far = list(far) + [diagonal(w) for w in sent]
    near_weights = [*own, *other, *across]

    normed, hidden1, slope1, mixed, gates = call(
        forward_near,
        "forward_near",
        arriving // tile,
        [tiles(x, tile)] + [whole(a) for a in (gain, bias, center, *near_weights)]
        + [(mark, "out", None)],
        [
            rows_out((arriving, width), BF16, tile),
            rows_out((arriving, 3 * units), BF16, tile),
            rows_out((arriving, 3 * units), BF16, tile),
            rows_out((arriving, width), F32, tile),
            rows_out((arriving, 128), F32, tile),
        ],
    )
    normed, *far = lax.optimization_barrier((normed, *far))
    last = [diagonal(after(w, normed)) for w in later]
    some = ((arriving, units), BF16, (tile, ends[2]), lambda i: (i, 0))
    hidden2, slope2, mixed = call(
        forward_more,
        "forward_more",
        arriving // tile,
        [tiles(normed, tile), tiles(mixed, tile)] + [whole(w) for w in far],
        [some, some, rows_out((arriving, width), F32, tile)],
    )
    far += last
    some = ((arriving, units), BF16, (tile, units - ends[2]), lambda i: (i, ends[2] // (units - ends[2])))
    hidden2, slope2, gated = call(
        forward_last,
        "forward_last",
        arriving // tile,
        [tiles(normed, tile), tiles(mixed, tile), tiles(gates, tile)]
        + [whole(w) for w in last]
        + [(hidden2, "out", None), (slope2, "out", None)],
        [some, some, rows_out((arriving, width), BF16, tile)],
        input_output_aliases={5: 0, 6: 1},
    )
    gated, dy = lax.optimization_barrier((gated, dy))
    returned = exchange(gated)

    def block_in(near, far, number):
        return (near, number) if number < 3 else (far, number - 3)

    def out_part(number, dtype):
        left = block_in(hidden1, hidden2, number)
        return weight_grad(left, (mixed_grad, 0), units, width, dtype, "out_weight_grad")

    def in_part(number, dtype, apart=False):
        right = block_in(grad1, grad2, number)
        return weight_grad((normed, 0), right, width, units, dtype, "in_weight_grad", apart)

    out_sent, mixed_grad = first_weight_grad(hidden2, dy, gates, units, "out_weight_grad")
    out_sent = [out_part(2, BF16), out_sent]
    out_across = [over("sub", out_sent[0]), diagonal(out_sent[1])]
    grad1, grad2, expert_grad, sums = call(
        functools.partial(backward, ends),
        "backward",
        arriving // tile,
        [tiles(a, tile) for a in (x, after(dy, *out_sent), gated, slope1, slope2, gates)]
        + [whole(a) for a in (gain, center)]
        + [(a, "out", None) for a in (*near_weights, *far)],
        [
            rows_out((arriving, 3 * units), BF16, tile),
            rows_out((arriving, units), BF16, tile),
            rows_out((arriving, width), BF16, tile),
            ((8, width), F32, (8, width), lambda i: (0, 0)),
        ],
        scratch_shapes=[
            pltpu.VMEM((width, 4 * units), BF16),
            pltpu.VMEM((4 * units, width), BF16),
            pltpu.SemaphoreType.DMA((12,)),
        ],
    )
    grad2, out_across[1] = lax.optimization_barrier((grad2, out_across[1]))
    in_sent = [in_part(3, BF16), in_part(2, BF16)]
    out_sent = out_part(1, BF16)
    moved = [over("sub", sums), over("half", sums), diagonal(sums)]
    expert_grad, returned, hidden1, in_sent[0], in_sent[1], out_sent, *moved = lax.optimization_barrier(
        (expert_grad, returned, hidden1, *in_sent, out_sent, *out_across, *moved)
    )
    out_across, moved = moved[:2], moved[2:]
    back = exchange(expert_grad)
    in_across = [over("sub", in_sent[1]), diagonal(in_sent[0])]
    out_beside = over("half", out_sent)
    in_beside = [over("half", p) for p in in_part(1, BF16, apart=True)]
    layer_out = taken_back(tokens, slot[:, None], returned, BF16, "layer_out")
    out_wgrad = sums_into(1 - half, [out_across[1], out_beside], None, "out_weight_grad_other")
    out_wgrad = sums_into(half, [out_part(0, F32), out_across[0]], out_wgrad, "out_weight_grad_own")
    in_own, layer_out, out_wgrad = lax.optimization_barrier((in_part(0, F32), layer_out, out_wgrad))
    in_wgrad = sums_into(1 - half, [in_across[1], in_beside], None, "in_weight_grad_other")
    in_wgrad, tokens_grad = finish(half, in_own, in_across[0], in_wgrad, cotangent, slot[:, None], back)
    kept, other_sums = sums + moved[0], moved[1] + moved[2]
    small = jnp.where((jnp.arange(halves) == half)[:, None, None], kept[None], other_sums[None])
    return (layer_out, tokens_grad, small[:, 0], small[:, 1], small[:, 2], in_wgrad, out_wgrad)


def solution(mesh):
    groups, tensor = mesh.shape["expert"], mesh.shape["tensor"]
    halves = 2
    split = Mesh(
        mesh.devices.reshape(groups, tensor // halves, halves), ("expert", "sub", "half")
    )
    rows, within = P(("expert", "sub", "half"), None), P("expert", None)
    columns = P("expert", None, ("sub", "half"))
    depth = P("expert", ("sub", "half"), None)
    return jax.shard_map(
        per_device,
        mesh=split,
        in_specs=(rows, rows, rows, within, within, within, columns, depth),
        out_specs=(rows, rows, within, within, within, columns, depth),
        check_vma=False,
    )
```

```python
import functools

import jax
import jax.numpy as jnp
from jax import lax
from jax.experimental import pallas as pl
from jax.experimental.pallas import tpu as pltpu
from jax.sharding import Mesh
from jax.sharding import PartitionSpec as P

epsilon = 1e-05
F32 = jnp.float32
BF16 = jnp.bfloat16
LAST = (((1,), (1,)), ((), ()))
ROWS = (((0,), (0,)), ((), ()))
VMEM_LIMIT = 58 * 2**20
TILE = 512


def product(a, b, dims=(((1,), (0,)), ((), ()))):
    return lax.dot_general(a, b, dims, preferred_element_type=F32)


def standardize(x):
    centered = x - jnp.mean(x, axis=-1, keepdims=True)
    inverse = lax.rsqrt(jnp.mean(centered * centered, axis=-1, keepdims=True) + epsilon)
    return centered * inverse, inverse


def steps_of(weights):
    for first, second in weights:
        step = min(TILE, first.shape[1]) if first.shape[1] % TILE == 0 else first.shape[1]
        for start in range(0, first.shape[1], step):
            yield first[:, start : start + step], second[start : start + step, :]


def through(normed, weights, hidden_ref, slope_ref):
    total, at = None, 0
    for first, second in steps_of(weights):
        z = product(normed, first)
        cumul = 0.5 * (1.0 + lax.erf(z * 0.7071067811865476))
        density = jnp.exp(-0.5 * z * z) * 0.3989422804014327
        hidden = (z * cumul).astype(BF16)
        hidden_ref[:, at : at + z.shape[1]] = hidden
        slope_ref[:, at : at + z.shape[1]] = (cumul + z * density).astype(BF16)
        part = product(hidden, second)
        total = part if total is None else total + part
        at += z.shape[1]
    return total


def paired(refs):
    return list(zip(refs[::2], refs[1::2]))


def forward_near(x, gain, bias, center, *rest):
    weights, (normed, hidden, slope, mixed, gates) = paired(rest[:-6]), rest[-5:]
    values = x[...].astype(F32)
    rows = (standardize(values)[0] * gain[...] + bias[...]).astype(BF16)
    normed[...] = rows
    mixed[...] = through(rows, weights, hidden, slope)
    gate = jax.nn.sigmoid(jnp.sum(values * center[...], axis=-1, keepdims=True))
    gates[...] = jnp.broadcast_to(gate, gates.shape)


def forward_more(rows, near, *rest):
    weights, (hidden, slope, mixed) = paired(rest[:-3]), rest[-3:]
    mixed[...] = near[...] + through(rows[...], weights, hidden, slope)


def forward_last(rows, near, gates, first, second, kept_hidden, kept_slope, hidden, slope, gated):
    del kept_hidden, kept_slope
    whole = near[...] + through(rows[...], [(first, second)], hidden, slope)
    gated[...] = (gates[:, :1] * whole).astype(BF16)


def backward(ends, x, dy, gated, s1, s2, gates, gain, center, *rest):
    count = 6 + 2 * (len(ends) - 1)
    refs, (g1, g2, expert_grad, sums), (ins, outs, sems) = rest[:count], rest[count:-3], rest[-3:]
    units = outs.shape[0] // 4
    step = min(TILE, units)
    copies = []
    for number, (first, second) in enumerate(paired(refs)):
        columns = pl.ds(number * units if number < 3 else 3 * units + ends[number - 3], first.shape[1])
        copies += [
            (min(number, 3), pltpu.make_async_copy(second, outs.at[columns, :], sems.at[2 * number])),
            (4, pltpu.make_async_copy(first, ins.at[:, columns], sems.at[2 * number + 1])),
        ]
    copies.sort(key=lambda c: c[0])

    @pl.when(pl.program_id(0) == 0)
    def _():
        for _, copy in copies:
            copy.start()
        sums[...] = jnp.zeros_like(sums)

    rows = x[...].astype(F32)
    gate = gates[:, :1]
    upper = dy[...].astype(F32)
    mixed_grad = (gate * upper).astype(BF16)
    for block in range(5):

        @pl.when(pl.program_id(0) == 0)
        def _():
            for used, copy in copies:
                if used == block:
                    copy.wait()

        for at in range(block * units, min(block + 1, 4) * units, step):
            hidden_grad = product(mixed_grad, outs[at : at + step, :], LAST)
            slope, grad, at = (s1, g1, at) if block < 3 else (s2, g2, at - 3 * units)
            grad[:, at : at + step] = (hidden_grad * slope[:, at : at + step].astype(F32)).astype(BF16)
    total = product(g1[...], ins[:, : 3 * units], LAST) + product(g2[...], ins[:, 3 * units :], LAST)
    xhat, inverse = standardize(rows)
    logit_grad = jnp.sum(upper * gated[...].astype(F32), axis=-1, keepdims=True) * (1.0 - gate)
    u = total * gain[...]
    expert_grad[...] = (
        inverse
        * (u - jnp.mean(u, axis=-1, keepdims=True) - xhat * jnp.mean(u * xhat, axis=-1, keepdims=True))
        + logit_grad * center[...]
    ).astype(BF16)
    sums[0:1, :] += jnp.sum(total * xhat, axis=0, keepdims=True)
    sums[1:2, :] += jnp.sum(total, axis=0, keepdims=True)
    sums[2:3, :] += jnp.sum(logit_grad * rows, axis=0, keepdims=True)


def call(kernel, name, steps, ins, outs, **more):
    def spec(shape, block, index):
        if block == "out":
            return pl.BlockSpec(memory_space=pl.ANY)
        if block is None:
            return pl.BlockSpec(shape, lambda *_: (0,) * len(shape), pipeline_mode=pl.Buffered(1))
        return pl.BlockSpec(block, index)

    return pl.pallas_call(
        kernel,
        grid=(steps,),
        in_specs=[spec(a.shape, block, index) for a, block, index in ins],
        out_specs=[pl.BlockSpec(block, index) for _, _, block, index in outs],
        out_shape=[jax.ShapeDtypeStruct(shape, dtype) for shape, dtype, _, _ in outs],
        compiler_params=pltpu.CompilerParams(vmem_limit_bytes=VMEM_LIMIT),
        cost_estimate=pl.CostEstimate(flops=1000, transcendentals=0, bytes_accessed=1000),
        name=name,
        **more,
    )(*[a for a, _, _ in ins])


def tiles(array, tile):
    return array, (tile, array.shape[1]), lambda i: (i, 0)


def rows_out(shape, dtype, tile):
    return shape, dtype, (tile, shape[1]), lambda i: (i, 0)


def whole(array):
    return array, None, None


def weight_grad(left, right, units, width, dtype, name, apart=False):
    (a, i), (b, j) = left, right
    tile = min(TILE, units)
    steps = units // tile

    def kernel(a, b, *outs):
        total = product(a[...], b[...], ROWS).astype(dtype)
        if not apart:
            outs[0][...] = total
        for n in range(steps if apart else 0):

            @pl.when(pl.program_id(0) == n)
            def _():
                outs[n][...] = total

    ins = [
        (a, (a.shape[0], tile), lambda n: (0, i * steps + n)),
        (b, (b.shape[0], width), lambda n: (0, j)),
    ]
    if apart:
        return call(kernel, name, steps, ins, [((tile, width), dtype, (tile, width), lambda n: (0, 0))] * steps)
    return call(kernel, name, steps, ins, [rows_out((units, width), dtype, tile)])[0]


def first_weight_grad(hidden, dy, gates, units, name):
    count, width = dy.shape
    tile = min(TILE, units)

    def kernel(a, dy, gates, out, mixed_grad):
        @pl.when(pl.program_id(0) == 0)
        def _():
            mixed_grad[...] = (gates[:, :1] * dy[...].astype(F32)).astype(BF16)

        out[...] = product(a[...], mixed_grad[...], ROWS).astype(BF16)

    return call(
        kernel,
        name,
        units // tile,
        [(hidden, (count, tile), lambda n: (0, n)), whole(dy), whole(gates)],
        [rows_out((units, width), BF16, tile), ((count, width), BF16, (count, width), lambda n: (0, 0))],
    )


def sums_into(number, operands, held, name):
    count, width = operands[0].shape
    tile = min(256, count)
    flat, ends = [], []
    for o in operands:
        pieces = o if isinstance(o, list) else [o]
        at = 0
        for p in pieces:
            flat.append(p)
            ends.append((at, at + p.shape[0] // tile))
            at += p.shape[0] // tile

    def kernel(number, *refs):
        out = refs[-1]
        step, total = pl.program_id(0), None
        for ref, (start, end) in zip(refs, ends):
            part = ref[...].astype(F32)
            if (start, end) != (0, count // tile):
                part = jnp.where((step >= start) & (step < end), part, 0.0)
            total = part if total is None else total + part
        out[0] = total

    def rows(start, end):
        return pl.BlockSpec((tile, width), lambda i, _: (jnp.clip(i - start, 0, end - start - 1), 0))

    extra = [] if held is None else [held]
    return pl.pallas_call(
        kernel,
        grid_spec=pltpu.PrefetchScalarGridSpec(
            num_scalar_prefetch=1,
            grid=(count // tile,),
            in_specs=[rows(*e) for e in ends] + [pl.BlockSpec(memory_space=pl.ANY)] * len(extra),
            out_specs=pl.BlockSpec((1, tile, width), lambda i, number: (number[0], i, 0)),
        ),
        out_shape=jax.ShapeDtypeStruct((2, count, width), F32),
        input_output_aliases={1 + len(flat): 0} if extra else {},
        compiler_params=pltpu.CompilerParams(vmem_limit_bytes=VMEM_LIMIT),
        cost_estimate=pl.CostEstimate(flops=1000, transcendentals=0, bytes_accessed=1000),
        name=name,
    )(number.astype(jnp.int32)[None], *flat, *extra)


def taken_back(base, slot, arrived, dtype, name):
    count, width = base.shape
    tile = min(512, count)

    def kernel(base, slot, arrived, out):
        slots = lax.broadcasted_iota(jnp.int32, (tile, arrived.shape[0]), 1)
        chosen = jnp.where(slot[...] == slots, 1.0, 0.0).astype(BF16)
        out[...] = (base[...].astype(F32) + product(chosen, arrived[...])).astype(dtype)

    return call(
        kernel,
        name,
        count // tile,
        [tiles(base, tile), tiles(slot, tile), whole(arrived)],
        [rows_out((count, width), dtype, tile)],
    )[0]


def finish(number, own, across, held, base, slot, arrived, steps=2):
    count, width = own.shape
    tile, tokens = count // steps, base.shape[0] // steps

    def kernel(number, own, across, base, slot, arrived, held, grad, out):
        slots = lax.broadcasted_iota(jnp.int32, (tokens, arrived.shape[0]), 1)
        chosen = jnp.where(slot[...] == slots, 1.0, 0.0).astype(BF16)
        out[...] = base[...].astype(F32) + product(chosen, arrived[...])
        grad[0] = own[...] + across[...].astype(F32)

    def rows(tile, width):
        return pl.BlockSpec((tile, width), lambda i, _: (i, 0))

    return pl.pallas_call(
        kernel,
        grid_spec=pltpu.PrefetchScalarGridSpec(
            num_scalar_prefetch=1,
            grid=(steps,),
            in_specs=[
                rows(tile, width),
                rows(tile, width),
                rows(tokens, base.shape[1]),
                rows(tokens, 1),
                pl.BlockSpec(arrived.shape, lambda i, _: (0, 0), pipeline_mode=pl.Buffered(1)),
                pl.BlockSpec(memory_space=pl.ANY),
            ],
            out_specs=[
                pl.BlockSpec((1, tile, width), lambda i, number: (number[0], i, 0)),
                rows(tokens, base.shape[1]),
            ],
        ),
        out_shape=[jax.ShapeDtypeStruct(held.shape, F32), jax.ShapeDtypeStruct(base.shape, F32)],
        input_output_aliases={6: 0},
        compiler_params=pltpu.CompilerParams(vmem_limit_bytes=VMEM_LIMIT),
        cost_estimate=pl.CostEstimate(flops=1000, transcendentals=0, bytes_accessed=1000),
        name="in_weight_grad_own_and_tokens_grad",
    )(number.astype(jnp.int32)[None], own, across, base, slot, arrived, held)


def waited(array):
    def kernel(array, out):
        out[...] = array[...].astype(F32)

    return pl.pallas_call(
        kernel,
        grid=(1,),
        in_specs=[pl.BlockSpec((16, 128), lambda i: (0, 0))],
        out_specs=pl.BlockSpec((16, 128), lambda i: (0, 0)),
        out_shape=jax.ShapeDtypeStruct((16, 128), F32),
        cost_estimate=pl.CostEstimate(flops=10**11, transcendentals=0, bytes_accessed=10**8),
        name="waited",
    )(array)


def after(value, *others):
    return lax.optimization_barrier((value, *others))[0]


def per_device(tokens, routes, cotangent, ln_gain, layer_norm_bias, centroid, w_in, w_out):
    groups, halves = lax.axis_size("expert"), lax.axis_size("half")
    half = lax.axis_index("half")
    experts = groups * halves
    count, width = tokens.shape
    capacity = 2 * count // experts
    arriving = experts * capacity
    units = w_in.shape[2]
    tile = min(TILE, arriving)
    targets = routes[:, 0]

    onehot = targets[:, None] == jnp.arange(experts, dtype=jnp.int32)[None, :]
    order = jnp.arange(count, dtype=jnp.int32)
    earlier = (order[:, None] >= order[None, :]).astype(BF16)
    ranks = jnp.dot(earlier, onehot.astype(BF16), preferred_element_type=F32)
    ranks = jnp.sum(jnp.where(onehot, ranks, 0.0), axis=1).astype(jnp.int32) - 1
    slot = targets * capacity + ranks
    slots = jnp.arange(arriving, dtype=jnp.int32)

    def place(values):
        chosen = (slots[:, None] == slot[None, :]).astype(BF16)
        return jnp.dot(chosen, values, preferred_element_type=F32).astype(BF16)

    def exchange(rows):
        rows = rows.reshape(experts, capacity, width)
        return lax.all_to_all(
            rows, ("expert", "half"), split_axis=0, concat_axis=0, tiled=True
        ).reshape(arriving, width)

    def over(axis, value):
        size = lax.axis_size(axis)
        return lax.ppermute(value, axis, [(i, size - 1 - i) for i in range(size)])

    def diagonal(value):
        return lax.ppermute(value, ("sub", "half"), [(i, 3 - i) for i in range(4)])

    def pick(stacked, index):
        return lax.dynamic_index_in_dim(stacked, index, 0, keepdims=False)

    gain = pick(ln_gain, half).astype(F32)[None, :]
    bias = pick(layer_norm_bias, half).astype(F32)[None, :]
    center = pick(centroid, half).astype(F32)[None, :]

    own = [pick(w_in, half), pick(w_out, half)]
    other = [pick(over("half", w), half) for w in (w_in, w_out)]
    across = [over("sub", w) for w in own]
    ends = [0, units // 8, units * 3 // 4, units]

    def piece(number):
        start, end = ends[number : number + 2]
        first = lax.dynamic_slice(w_in, (1 - half, 0, start), (1, width, end - start))
        return [first[0], lax.dynamic_slice(w_out, (1 - half, start, 0), (1, end - start, width))[0]]

    mark = waited(across[0])
    far = [diagonal(after(w, mark)) for w in piece(0)]
    x = exchange(place(tokens))
    sent = [*piece(1), *piece(2)]
    x, dy_sent, mark, *arrived = lax.optimization_barrier(
        (x, place(cotangent), mark, *own, *other, *across, *far, *sent)
    )
    own, other, across, far, sent = (arrived[n : n + 2] for n in (0, 2, 4, 6, 8))
    later = arrived[10:]
    dy = exchange(dy_sent)
    far = list(far) + [diagonal(w) for w in sent]
    near_weights = [*own, *other, *across]

    normed, hidden1, slope1, mixed, gates = call(
        forward_near,
        "forward_near",
        arriving // tile,
        [tiles(x, tile)] + [whole(a) for a in (gain, bias, center, *near_weights)]
        + [(mark, "out", None)],
        [
            rows_out((arriving, width), BF16, tile),
            rows_out((arriving, 3 * units), BF16, tile),
            rows_out((arriving, 3 * units), BF16, tile),
            rows_out((arriving, width), F32, tile),
            rows_out((arriving, 128), F32, tile),
        ],
    )
    normed, *far = lax.optimization_barrier((normed, *far))
    last = [diagonal(after(w, normed)) for w in later]
    some = ((arriving, units), BF16, (tile, ends[2]), lambda i: (i, 0))
    hidden2, slope2, mixed = call(
        forward_more,
        "forward_more",
        arriving // tile,
        [tiles(normed, tile), tiles(mixed, tile)] + [whole(w) for w in far],
        [some, some, rows_out((arriving, width), F32, tile)],
    )
    far += last
    large = min(2 * TILE, arriving)
    some = ((arriving, units), BF16, (large, units - ends[2]), lambda i: (i, ends[2] // (units - ends[2])))
    hidden2, slope2, gated = call(
        forward_last,
        "forward_last",
        arriving // large,
        [tiles(normed, large), tiles(mixed, large), tiles(gates, large)]
        + [whole(w) for w in last]
        + [(hidden2, "out", None), (slope2, "out", None)],
        [some, some, rows_out((arriving, width), BF16, large)],
        input_output_aliases={5: 0, 6: 1},
    )
    gated, dy = lax.optimization_barrier((gated, dy))
    returned = exchange(gated)

    def block_in(near, far, number):
        return (near, number) if number < 3 else (far, number - 3)

    def out_part(number, dtype):
        left = block_in(hidden1, hidden2, number)
        return weight_grad(left, (mixed_grad, 0), units, width, dtype, "out_weight_grad")

    def in_part(number, dtype, apart=False):
        right = block_in(grad1, grad2, number)
        return weight_grad((normed, 0), right, width, units, dtype, "in_weight_grad", apart)

    out_sent, mixed_grad = first_weight_grad(hidden2, dy, gates, units, "out_weight_grad")
    out_sent = [out_part(2, BF16), out_sent]
    out_across = [over("sub", out_sent[0]), diagonal(out_sent[1])]
    grad1, grad2, expert_grad, sums = call(
        functools.partial(backward, ends),
        "backward",
        arriving // tile,
        [tiles(a, tile) for a in (x, after(dy, *out_sent), gated, slope1, slope2, gates)]
        + [whole(a) for a in (gain, center)]
        + [(a, "out", None) for a in (*near_weights, *far)],
        [
            rows_out((arriving, 3 * units), BF16, tile),
            rows_out((arriving, units), BF16, tile),
            rows_out((arriving, width), BF16, tile),
            ((8, width), F32, (8, width), lambda i: (0, 0)),
        ],
        scratch_shapes=[
            pltpu.VMEM((width, 4 * units), BF16),
            pltpu.VMEM((4 * units, width), BF16),
            pltpu.SemaphoreType.DMA((12,)),
        ],
    )
    grad2, out_across[1] = lax.optimization_barrier((grad2, out_across[1]))
    in_sent = [in_part(3, BF16), in_part(2, BF16)]
    out_sent = out_part(1, BF16)
    moved = [over("sub", sums), over("half", sums), diagonal(sums)]
    expert_grad, returned, hidden1, in_sent[0], in_sent[1], out_sent, *moved = lax.optimization_barrier(
        (expert_grad, returned, hidden1, *in_sent, out_sent, *out_across, *moved)
    )
    out_across, moved = moved[:2], moved[2:]
    back = exchange(expert_grad)
    in_across = [over("sub", in_sent[1]), diagonal(in_sent[0])]
    out_beside = over("half", out_sent)
    in_beside = [over("half", p) for p in in_part(1, BF16, apart=True)]
    layer_out = taken_back(tokens, slot[:, None], returned, BF16, "layer_out")
    out_wgrad = sums_into(1 - half, [out_across[1], out_beside], None, "out_weight_grad_other")
    out_wgrad = sums_into(half, [out_part(0, F32), out_across[0]], out_wgrad, "out_weight_grad_own")
    in_own, layer_out, out_wgrad = lax.optimization_barrier((in_part(0, F32), layer_out, out_wgrad))
    in_wgrad = sums_into(1 - half, [in_across[1], in_beside], None, "in_weight_grad_other")
    in_wgrad, tokens_grad = finish(half, in_own, in_across[0], in_wgrad, cotangent, slot[:, None], back)
    kept, other_sums = sums + moved[0], moved[1] + moved[2]
    small = jnp.where((jnp.arange(halves) == half)[:, None, None], kept[None], other_sums[None])
    return (layer_out, tokens_grad, small[:, 0], small[:, 1], small[:, 2], in_wgrad, out_wgrad)


def solution(mesh):
    groups, tensor = mesh.shape["expert"], mesh.shape["tensor"]
    halves = 2
    split = Mesh(
        mesh.devices.reshape(groups, tensor // halves, halves), ("expert", "sub", "half")
    )
    rows, within = P(("expert", "sub", "half"), None), P("expert", None)
    columns = P("expert", None, ("sub", "half"))
    depth = P("expert", ("sub", "half"), None)
    return jax.shard_map(
        per_device,
        mesh=split,
        in_specs=(rows, rows, rows, within, within, within, columns, depth),
        out_specs=(rows, rows, within, within, within, columns, depth),
        check_vma=False,
    )
```
